32 devices in a mesh: gx: 4 (over x, core), gy: 4 (over z), gz: 2 (over y).
Axes of the slice: x: 2, y: 2, z: 4, core: 2. Of those that a mesh axis runs over, the one named last changes fastest.
Arguments:
- features: bfloat16 [4096, 25, 128], P(('gx', 'gy', 'gz')), may hold values from -6 to 6
- positions: bfloat16 [3, 4096], P(None, ('gx', 'gy', 'gz')), may hold values from 0 to 4
- probe_positions: float32 [3, 8192], P(None, ('gx', 'gy', 'gz')), may hold values from 0 to 4
- neighbours: int32 [4096, 20], P(('gx', 'gy', 'gz')), may hold values from 0 to 235
- routes: int32 [4096, 1], P(('gx', 'gy', 'gz')), may hold values from 0 to 7; in each aligned block of 128 rows (0 to 127, 128 to 255, ...) at most 32 rows name the same one
- pattern: int32 [64, 8], P(('gx', 'gy', 'gz')), may hold values 0 or 1
- charge_index: int32 [1], replicated, may hold values from 0 to 7
- charge_table: bfloat16 [8, 128], replicated, may hold values from -6 to 6
- w_radial_in: bfloat16 [8, 64], replicated, may hold values from -2 to 2
- w_radial_out: bfloat16 [64, 1280], replicated, may hold values from -0.75 to 0.75
- w_mix: bfloat16 [5, 128, 128], replicated, may hold values from -0.5 to 0.5
- w_self: bfloat16 [5, 128, 128], replicated, may hold values from -0.5 to 0.5
- w_gate: bfloat16 [128, 512], replicated, may hold values from -0.5 to 0.5
- w_read: bfloat16 [8, 5, 128], replicated, may hold values from -0.5 to 0.5
Outputs:
- atoms_out: bfloat16 [4096, 25, 128], P(('gx', 'gy', 'gz'))
- density: float32 [8192], P(('gx', 'gy', 'gz'))
The draws below stay inside these ranges and needn't reach their ends.
Inputs may be any that keep to these rules, and one draw needn't show every extreme that they name: In box (i, j, k) an index n >= 128 names a front atom of the box or of one of its 26 periodic neighbours, coded as in the reference program. `routes`: A tile number t is gy index times 2 plus gz index within the atom's gx plane; the rows of one box name each tile at most 32 times and name different tiles in one row.
All inputs are finite; a program needn't handle non-finite values. No bound on the sum of `pattern` on one device may be relied on, other than what follows from the above.
Results may differ from the reference program's by a relative error of at most 0.0031.
Values may be sent and summed in bfloat16 or wider, within the bound.
No kernel may reach another device: no remote copies, remote signals or barrier semaphores. Data moves between devices by JAX's collectives and lax.ppermute only.
A program may use at most 64 MiB of HBM per device.

```python
import math
import jax
import jax.numpy as jnp
import numpy as np
from jax import lax

CH = 128
LMAX = 4
IRREPS = 25
NB = 8
RH = 64
K = 20
ATOMS_DEV = 128
BND = 4
PROBE_DEV = 256
PB = 128
NQ = 8
TOPC = 1
NSRC = 8
CAP = 32
ATOMS = 4096
PROBES = 8192
PBLOCKS = 64
N_GX = 4
N_GY = 4
N_GZ = 2


def set_ends(entries, rng, low, top_value):
    longest = entries.shape.index(max(entries.shape))
    spots = []
    for shift in (0, 1):
        where = [jax.random.randint(jax.random.fold_in(rng, axis), (), 0, length) for axis, length in enumerate(entries.shape)]
        where[longest] = (where[longest] + shift) % entries.shape[longest]
        spots.append(tuple(where))
    return entries.at[spots[0]].set(low).at[spots[1]].set(top_value)


def block_levels(stream_key, shape, split, low, high):
    level = 1.0
    for dim, parts in split:
        draws = jax.random.uniform(jax.random.fold_in(jax.random.fold_in(stream_key, 6), dim), (parts,), jnp.float32, low / len(split), high / len(split))
        level = level * jnp.repeat(jnp.exp(draws), shape[dim] // parts).reshape((-1,) + (1,) * (len(shape) - 1 - dim))
    return level


def routed_block(key, own, number, rows, count, top, most, slope):
    sequence = jax.random.permutation(key, count)
    heavy_load, ordinary = portions_of(count, rows * top, most, slope, True), portions_of(count, rows * top, most, slope, False)
    places = jnp.arange(count)

    def named(lengths, turn):
        used = int((lengths > 0).sum())
        fixed = max(1, used // 4)
        shifted = fixed + (places - fixed + turn * (used - fixed)) % max(1, count - fixed)
        return jnp.zeros((count,), jnp.int32).at[sequence[jnp.where(places < fixed, places, shifted)]].set(jnp.asarray(lengths, jnp.int32))

    lengths = jnp.where(number % 4 == 0, named(heavy_load, number // 4), named(ordinary, number - number // 4 - 1))
    mixed = jax.random.permutation(jax.random.fold_in(own, 3), count)
    source_of, sink = mixed[0:count // 2 * 2:2], mixed[1:count // 2 * 2:2]
    room = jnp.minimum(lengths[source_of] - 1, most - lengths[sink]) // 2
    room = jnp.where((source_of == sequence[0]) | (sink == sequence[0]) | (lengths[sink] == 0), 0, jnp.maximum(room, 0))
    shifted = jax.random.randint(jax.random.fold_in(own, 4), (count // 2,), 0, 1 << 20) % (room + 1)
    lengths = lengths.at[source_of].add(-shifted).at[sink].add(shifted)
    items = jnp.searchsorted(jnp.cumsum(lengths), jnp.arange(rows * top), side="right").astype(jnp.int32)
    listing = items.reshape(top, rows).T
    listing = listing[jax.random.permutation(jax.random.fold_in(own, 1), rows)]
    turn = jax.random.randint(jax.random.fold_in(own, 2), (rows, 1), 0, top)
    return jnp.take_along_axis(listing, (jnp.arange(top)[None, :] + turn) % top, axis=1)


def portions_of(amount, total, bound, skew, full):
    portions = [(1 << 20) // math.isqrt(rank ** skew) + 1 for rank in range(1, amount + 1)]
    largest = bound if full else min(bound, max(-(-total // amount), total * portions[0] // sum(portions)))
    least = 1 if total - largest >= amount - 1 else 0
    holding, surplus = [largest] + [least] * (amount - 1), total - largest - least * (amount - 1)
    while surplus > 0:
        candidates = [i for i in range(1, amount) if holding[i] < largest] or [i for i in range(1, amount) if holding[i] < bound]
        whole, left = sum([portions[i] for i in candidates]), surplus
        for i in candidates:
            more = min(bound - holding[i], max(1, left * portions[i] // whole), surplus)
            holding[i] = holding[i] + more
            surplus = surplus - more
    return np.array(holding)


def scatter_about(stream_key, dims, width, reach, cuts=(), dtype=jnp.bfloat16):
    drawn = width * jax.random.normal(stream_key, dims, jnp.float32)
    if cuts:
        drawn = drawn * block_levels(stream_key, dims, cuts, -0.22, 0.18)
    return jnp.clip(drawn, -reach, reach).astype(dtype)


def setup_inputs(seed: int = 0) -> dict:
    streams_of = jax.random.split(jax.random.key(seed), 15)
    features = scatter_about(streams_of[0], (ATOMS, IRREPS, CH), 1.0, 6.0, ((0, 32),))
    positions = jnp.clip(4.0 * jax.random.uniform(streams_of[1], (3, ATOMS), jnp.float32) ** block_levels(streams_of[1], (3, ATOMS), ((1, 32),), -0.2, 0.2), 0.0, 4.0).astype(jnp.bfloat16)
    probe_positions = jnp.clip(4.0 * jax.random.uniform(streams_of[2], (3, PROBES), jnp.float32) ** block_levels(streams_of[2], (3, PROBES), ((1, 32),), -0.2, 0.2), 0.0, 4.0)
    neighbours = set_ends(jax.random.randint(streams_of[3], (ATOMS, K), 0, ATOMS_DEV + 27 * BND), jax.random.fold_in(streams_of[3], 1), 0, (ATOMS_DEV + 27 * BND) - 1).astype(jnp.int32)
    routes_keys = jax.random.split(jax.random.fold_in(streams_of[4], 1), ATOMS // ATOMS_DEV)
    routes_turns = jax.random.permutation(jax.random.fold_in(streams_of[4], 3), ATOMS // ATOMS_DEV)
    routes = jax.vmap(lambda own, number: routed_block(jax.random.fold_in(streams_of[4], 2), own, number, ATOMS_DEV, N_GY * N_GZ, TOPC, CAP, 2))(routes_keys, routes_turns).reshape((ATOMS, TOPC))
    pattern = set_ends((jax.random.randint(streams_of[5], (PBLOCKS, NSRC), 0, 2) < 1).astype(jnp.int32), jax.random.fold_in(streams_of[5], 1), 0, 1)
    charge_index = jax.random.randint(streams_of[6], (1,), 0, NQ).astype(jnp.int32)
    charge_table = scatter_about(streams_of[7], (NQ, CH), 1.0, 6.0)
    w_radial_in = scatter_about(streams_of[8], (NB, RH), NB ** -0.5, 2.0)
    w_radial_out = scatter_about(streams_of[9], (RH, 2 * (LMAX + 1) * CH), RH ** -0.5, 0.75)
    w_mix = scatter_about(streams_of[10], (LMAX + 1, CH, CH), CH ** -0.5, 0.5)
    w_self = scatter_about(streams_of[11], (LMAX + 1, CH, CH), CH ** -0.5, 0.5)
    w_gate = scatter_about(streams_of[12], (CH, LMAX * CH), CH ** -0.5, 0.5)
    w_read = scatter_about(streams_of[13], (NB, LMAX + 1, CH), CH ** -0.5, 0.5)
    return dict(features=features, positions=positions, probe_positions=probe_positions, neighbours=neighbours, routes=routes, pattern=pattern, charge_index=charge_index, charge_table=charge_table, w_radial_in=w_radial_in, w_radial_out=w_radial_out, w_mix=w_mix, w_self=w_self, w_gate=w_gate, w_read=w_read)


CUTOFF = 8.0
WIDTH_R = 0.75
REACH = 6.0
FLOOR = 0.25

def harmonics(comp_x, comp_y, comp_z):
    sq_x = comp_x * comp_x
    sq_y = comp_y * comp_y
    sq_z = comp_z * comp_z
    return jnp.stack([jnp.ones_like(comp_x), math.sqrt(3.0) * comp_y, math.sqrt(3.0) * comp_z, math.sqrt(3.0) * comp_x, math.sqrt(15.0) * comp_x * comp_y, math.sqrt(15.0) * comp_y * comp_z, 0.5 * math.sqrt(5.0) * (3.0 * sq_z - 1.0), math.sqrt(15.0) * comp_x * comp_z, 0.5 * math.sqrt(15.0) * (sq_x - sq_y), math.sqrt(35.0 / 8.0) * comp_y * (3.0 * sq_x - sq_y), math.sqrt(105.0) * comp_x * comp_y * comp_z, math.sqrt(21.0 / 8.0) * comp_y * (5.0 * sq_z - 1.0), 0.5 * math.sqrt(7.0) * comp_z * (5.0 * sq_z - 3.0), math.sqrt(21.0 / 8.0) * comp_x * (5.0 * sq_z - 1.0), 0.5 * math.sqrt(105.0) * comp_z * (sq_x - sq_y), math.sqrt(35.0 / 8.0) * comp_x * (sq_x - 3.0 * sq_y), 1.5 * math.sqrt(35.0) * comp_x * comp_y * (sq_x - sq_y), 1.5 * math.sqrt(17.5) * comp_y * comp_z * (3.0 * sq_x - sq_y), 1.5 * math.sqrt(5.0) * comp_x * comp_y * (7.0 * sq_z - 1.0), 1.5 * math.sqrt(2.5) * comp_y * comp_z * (7.0 * sq_z - 3.0), 0.375 * (35.0 * sq_z * sq_z - 30.0 * sq_z + 3.0), 1.5 * math.sqrt(2.5) * comp_x * comp_z * (7.0 * sq_z - 3.0), 0.75 * math.sqrt(5.0) * (sq_x - sq_y) * (7.0 * sq_z - 1.0), 1.5 * math.sqrt(17.5) * comp_x * comp_z * (sq_x - 3.0 * sq_y), 0.375 * math.sqrt(35.0) * (sq_x * sq_x - 6.0 * sq_x * sq_y + sq_y * sq_y)])

def radial_basis(distance, functions):
    centres = jnp.arange(functions).astype(jnp.float32) * (REACH / (functions - 1))
    bcast_shape = (functions,) + (1,) * distance.ndim
    envelope = jnp.square(1.0 - jnp.square(distance / CUTOFF))
    return jnp.exp(-jnp.square((distance[None] - centres.reshape(bcast_shape)) / WIDTH_R)) * envelope[None]

def geometry(offset_vec):
    distance = jnp.sqrt(lax.optimization_barrier(jnp.sum(offset_vec * offset_vec, axis=0)))
    direction = offset_vec / jnp.maximum(distance, FLOOR)[None]
    return (distance, harmonics(direction[0], direction[1], direction[2]))

def embed(features, charge_index, charge_table):
    levels = charge_table.shape[0]
    chosen = (jnp.arange(levels).astype(jnp.int32) == charge_index[0]).astype(jnp.float32)
    charge_shift = lax.optimization_barrier(jnp.sum(chosen[:, None] * charge_table.astype(jnp.float32), axis=0))
    scalar = (features[:, 0:1, :].astype(jnp.float32) + charge_shift[None, None, :]).astype(jnp.bfloat16)
    return jnp.concatenate([scalar, features[:, 1:, :]], axis=1)

def aggregate(feats_all, pos_all, neighbours, own_pos, w_radial_in, w_radial_out):
    row_count, fanout = neighbours.shape
    channels = feats_all.shape[-1]
    degrees = w_radial_out.shape[1] // (2 * channels)
    repeats = [2 * degree + 1 for degree in range(degrees)]
    components = degrees * degrees
    block_rows = 16

    def one_block(inputs):
        index_block, centre = inputs
        flat_index = index_block.reshape(-1)
        gathered = jnp.take(feats_all, flat_index, axis=0)
        offset_vec = (jnp.take(pos_all, flat_index, axis=0) - jnp.repeat(centre, fanout, axis=0)).T
        distance, angular = geometry(offset_vec)
        radial_in = radial_basis(distance, w_radial_in.shape[0]).T.astype(jnp.bfloat16)
        hidden = jax.nn.silu(jnp.dot(radial_in, w_radial_in, preferred_element_type=jnp.float32)).astype(jnp.bfloat16)
        radial = jnp.dot(hidden, w_radial_out, preferred_element_type=jnp.float32).reshape(-1, 2, degrees, channels)
        same_path = jnp.repeat(radial[:, 0], jnp.array(repeats), axis=1, total_repeat_length=components)
        cross_path = jnp.repeat(radial[:, 1], jnp.array(repeats), axis=1, total_repeat_length=components)
        values = gathered.astype(jnp.float32)
        message = same_path * values + cross_path * values[:, 0:1, :] * angular.T[:, :, None]
        return lax.optimization_barrier(jnp.sum(message.reshape(block_rows, fanout, components, channels), axis=1)) * (1.0 / math.sqrt(fanout))
    result = lax.map(one_block, (neighbours.reshape(row_count // block_rows, block_rows, fanout), own_pos.reshape(row_count // block_rows, block_rows, 3)))
    return result.reshape(row_count, components, channels).astype(jnp.bfloat16)

def update(embedded, aggregated, w_mix, w_self, w_gate):
    row_count, components, channels = embedded.shape
    degrees = w_mix.shape[0]
    gate_values = jax.nn.sigmoid(jnp.dot(aggregated[:, 0, :], w_gate, preferred_element_type=jnp.float32))
    gate_values = gate_values.reshape(row_count, degrees - 1, channels)
    pieces = []
    for degree in range(degrees):
        lower_end = degree * degree
        upper_end = lower_end + 2 * degree + 1
        mixed_term = jnp.dot(aggregated[:, lower_end:upper_end, :].reshape(-1, channels), w_mix[degree], preferred_element_type=jnp.float32)
        mixed_term = mixed_term + jnp.dot(embedded[:, lower_end:upper_end, :].reshape(-1, channels), w_self[degree], preferred_element_type=jnp.float32)
        mixed_term = mixed_term.reshape(row_count, upper_end - lower_end, channels)
        residual_part = embedded[:, lower_end:upper_end, :].astype(jnp.float32)
        if degree == 0:
            pieces.append(residual_part + jax.nn.silu(mixed_term))
        else:
            pieces.append(residual_part + mixed_term * gate_values[:, degree - 1][:, None, :])
    return jnp.concatenate(pieces, axis=1).astype(jnp.bfloat16)

def readout(features, w_read):
    row_count, components, channels = features.shape
    degrees = w_read.shape[1]
    pieces = []
    for degree in range(degrees):
        lower_end = degree * degree
        upper_end = lower_end + 2 * degree + 1
        partial_value = jnp.dot(features[:, lower_end:upper_end, :].reshape(-1, channels), w_read[:, degree, :].T, preferred_element_type=jnp.float32)
        pieces.append(partial_value.reshape(row_count, upper_end - lower_end, -1))
    return jnp.transpose(jnp.concatenate(pieces, axis=1), (0, 2, 1))

def slot_rows(routes, dests, capacity):
    row_count, cover_count = routes.shape
    flat_dest = routes.reshape(-1).astype(jnp.int32)
    onehot = (flat_dest[:, None] == jnp.arange(dests).astype(jnp.int32)[None, :]).astype(jnp.int32)
    rank_in_dest = lax.optimization_barrier(jnp.sum((jnp.cumsum(onehot, axis=0) - 1) * onehot, axis=1)).astype(jnp.int32)
    slot_index = flat_dest * capacity + rank_in_dest
    source_row = (jnp.arange(row_count * cover_count) // cover_count).astype(jnp.int32)
    return jnp.full((dests * capacity,), row_count, jnp.int32).at[slot_index].set(source_row)

def density_tile(probe_pos, pattern, slot_pos, slot_coeffs, capacity, probe_block):
    slot_count = slot_pos.shape[0]
    probe_count = probe_pos.shape[1]
    span = 128 if slot_count % 128 == 0 else slot_count
    keep_mask = jnp.repeat(jnp.repeat(pattern.astype(jnp.float32), probe_block, axis=0), capacity, axis=1)

    def one_span(total, start):
        where_pos = lax.dynamic_slice_in_dim(slot_pos, start, span, 0)
        coeffs = lax.dynamic_slice_in_dim(slot_coeffs, start, span, 0)
        keep = lax.dynamic_slice_in_dim(keep_mask, start, span, 1)
        offset_vec = probe_pos[:, :, None] - where_pos.T[:, None, :]
        distance, angular = geometry(offset_vec)
        radial_in = radial_basis(distance, coeffs.shape[1])
        contracted = jnp.einsum('lps,sbl->bps', angular, coeffs, precision=lax.Precision.HIGHEST)
        return (total + lax.optimization_barrier(jnp.sum(lax.optimization_barrier(jnp.sum(radial_in * contracted, axis=0)) * keep, axis=1)), None)
    starts = jnp.arange(0, slot_count, span).astype(jnp.int32)
    total, unused = lax.scan(one_span, jnp.zeros((probe_count,), jnp.float32), starts)
    return total * (1.0 / math.sqrt(slot_count))

def reference(features, positions, probe_positions, neighbours, routes, pattern, charge_index, charge_table, w_radial_in, w_radial_out, w_mix, w_self, w_gate, w_read):
    devices_all = N_GX * N_GY * N_GZ
    plane = N_GY * N_GZ
    per_dev = ATOMS_DEV
    rim = BND
    capacity = CAP
    embedded = embed(features, charge_index, charge_table)
    atom_pos = positions.astype(jnp.float32).T
    rim_feats = embedded.reshape(devices_all, per_dev, IRREPS, CH)[:, :rim]
    rim_pos = atom_pos.reshape(devices_all, per_dev, 3)[:, :rim]
    offsets = jnp.arange(27).astype(jnp.int32)
    off_x = offsets // 9 - 1
    off_y = offsets // 3 % 3 - 1
    off_z = offsets % 3 - 1

    def layer_one(device):
        pos_x = device // plane
        pos_y = device // N_GZ % N_GY
        pos_z = device % N_GZ
        sources = (pos_x + off_x) % N_GX * plane + (pos_y + off_y) % N_GY * N_GZ + (pos_z + off_z) % N_GZ
        ghost_feats = jnp.take(rim_feats, sources, axis=0).reshape(27 * rim, IRREPS, CH)
        ghost_pos = jnp.take(rim_pos, sources, axis=0).reshape(27 * rim, 3)
        own_feats = lax.dynamic_slice_in_dim(embedded, device * per_dev, per_dev, 0)
        own_pos = lax.dynamic_slice_in_dim(atom_pos, device * per_dev, per_dev, 0)
        own_lists = lax.dynamic_slice_in_dim(neighbours, device * per_dev, per_dev, 0)
        feats_all = jnp.concatenate([own_feats, ghost_feats], axis=0)
        pos_all = jnp.concatenate([own_pos, ghost_pos], axis=0)
        aggregated = aggregate(feats_all, pos_all, own_lists, own_pos, w_radial_in, w_radial_out)
        updated = update(own_feats, aggregated, w_mix, w_self, w_gate)
        return (updated, readout(updated, w_read))
    device_ids = jnp.arange(devices_all).astype(jnp.int32)
    updated_all, coeffs_all = lax.map(layer_one, device_ids)

    def table_one(route_block):
        return slot_rows(route_block, plane, capacity)
    tables = lax.map(table_one, routes.reshape(devices_all, per_dev, TOPC))
    flat_coeffs = jnp.concatenate([coeffs_all.reshape(-1, NB, IRREPS), jnp.zeros((1, NB, IRREPS), jnp.float32)], axis=0)
    flat_pos = jnp.concatenate([atom_pos, jnp.zeros((1, 3), jnp.float32)], axis=0)
    pattern_rows = PROBE_DEV // PB

    def tile_one(device):
        pos_x = device // plane
        target = device % plane
        sources = pos_x * plane + jnp.arange(plane).astype(jnp.int32)
        rows_here = lax.dynamic_slice_in_dim(jnp.take(tables, sources, axis=0), target * capacity, capacity, 1)
        global_rows = jnp.where(rows_here < per_dev, sources[:, None] * per_dev + rows_here, devices_all * per_dev).reshape(-1)
        slot_coeffs = jnp.take(flat_coeffs, global_rows, axis=0)
        slot_pos = jnp.take(flat_pos, global_rows, axis=0)
        probe_pos = lax.dynamic_slice_in_dim(probe_positions, device * PROBE_DEV, PROBE_DEV, 1)
        tile_pattern = lax.dynamic_slice_in_dim(pattern, device * pattern_rows, pattern_rows, 0)
        return density_tile(probe_pos, tile_pattern, slot_pos, slot_coeffs, capacity, PB)
    density = lax.map(tile_one, device_ids).reshape(-1)
    return (updated_all.reshape(ATOMS, IRREPS, CH), density)
```

```python
import functools
import math

import jax
import jax.numpy as jnp
from jax import lax
from jax.experimental import pallas as pl
from jax.experimental.pallas import tpu as pltpu
from jax.sharding import PartitionSpec as P

CUTOFF = 8.0
WIDTH_R = 0.75
REACH = 6.0
FLOOR = 0.25
PLANE = ("gy", "gz")
ROWS = 16
SUB = 8
HIGH = lax.Precision.HIGHEST


def harmonics(x, y, z):
    sx, sy, sz = x * x, y * y, z * z
    xy, yz, xz = x * y, y * z, x * z
    dif = sx - sy
    five, seven, seven3 = 5.0 * sz - 1.0, 7.0 * sz - 1.0, 7.0 * sz - 3.0
    tx, ty = sx - 3.0 * sy, 3.0 * sx - sy
    return [
        None,
        math.sqrt(3.0) * y,
        math.sqrt(3.0) * z,
        math.sqrt(3.0) * x,
        math.sqrt(15.0) * xy,
        math.sqrt(15.0) * yz,
        0.5 * math.sqrt(5.0) * (3.0 * sz - 1.0),
        math.sqrt(15.0) * xz,
        0.5 * math.sqrt(15.0) * dif,
        math.sqrt(35.0 / 8.0) * y * ty,
        math.sqrt(105.0) * xy * z,
        math.sqrt(21.0 / 8.0) * y * five,
        0.5 * math.sqrt(7.0) * z * (5.0 * sz - 3.0),
        math.sqrt(21.0 / 8.0) * x * five,
        0.5 * math.sqrt(105.0) * z * dif,
        math.sqrt(35.0 / 8.0) * x * tx,
        1.5 * math.sqrt(35.0) * xy * dif,
        1.5 * math.sqrt(17.5) * yz * ty,
        1.5 * math.sqrt(5.0) * xy * seven,
        1.5 * math.sqrt(2.5) * yz * seven3,
        0.375 * (35.0 * sz * sz - 30.0 * sz + 3.0),
        1.5 * math.sqrt(2.5) * xz * seven3,
        0.75 * math.sqrt(5.0) * dif * seven,
        1.5 * math.sqrt(17.5) * xz * tx,
        0.375 * math.sqrt(35.0) * (sx * sx - 6.0 * sx * sy + sy * sy),
    ]


def geometry(x, y, z):
    dist = jnp.sqrt(x * x + y * y + z * z)
    inv = 1.0 / jnp.maximum(dist, FLOOR)
    return dist, harmonics(x * inv, y * inv, z * inv)


def degree_of(component):
    return math.isqrt(component)


def nt_dot(a, b, precision=None):
    return lax.dot_general(
        a, b, (((1,), (1,)), ((), ())), precision=precision, preferred_element_type=jnp.float32
    )


def dot(a, b, precision=None):
    return jnp.dot(a, b, precision=precision, preferred_element_type=jnp.float32)


def layer_kernel(
    sizes,
    nbr_ref,
    own_ref,
    g0_ref,
    g1_ref,
    g2_ref,
    pos_ref,
    win_ref,
    wout_ref,
    wcat_ref,
    wgate_ref,
    wread_ref,
    probe_ref,
    tile_ref,
    out_ref,
    dens_ref,
    cand,
    post,
    agg,
    rad,
    coef,
    part,
):
    per_dev, channels, degrees, rim_rows, rim_pad, tiles, scale = sizes
    comps = degrees * degrees
    width = comps * channels
    kdim = cand.shape[0]
    fanout = nbr_ref.shape[1]
    step = pl.program_id(0)
    edges = ROWS * fanout
    sub_edges = SUB * fanout
    subs = ROWS // SUB
    f32, bf16 = jnp.float32, jnp.bfloat16

    @pl.when(step == 0)
    def _():
        cand[0:per_dev, :] = own_ref[...]
        pos_all = [pos_ref[...]]
        for g, ref in enumerate((g0_ref, g1_ref, g2_ref)):
            block = ref[...]
            if rim_pad > rim_rows:
                block = jnp.concatenate(
                    [block, jnp.zeros((rim_pad - rim_rows, width + channels), bf16)], axis=0
                )
            lo = per_dev + g * rim_pad
            cand[lo : lo + rim_pad, :] = block[:, :width]
            pos_all.append(block[:, width:].astype(f32))
        post[...] = jnp.transpose(jnp.concatenate(pos_all, axis=0))[0:SUB, :].astype(bf16)

    lane = lax.broadcasted_iota(jnp.int32, (SUB, kdim), 1)
    row = lax.broadcasted_iota(jnp.int32, (SUB, kdim), 0)
    hot, delta = [], []
    for s in range(subs):
        index = nbr_ref[s * SUB : (s + 1) * SUB, :]
        centre = jnp.where(lane == row + (step * ROWS + s * SUB), 1.0, 0.0)
        for k in range(fanout):
            one = jnp.where(lane == index[:, k : k + 1], 1.0, 0.0)
            hot.append(one)
            delta.append(one - centre)
    hot = jnp.concatenate(hot, axis=0).astype(bf16)
    delta = jnp.concatenate(delta, axis=0).astype(bf16)
    offset = nt_dot(post[...], delta)
    dist, angular = geometry(offset[0:1], offset[1:2], offset[2:3])
    functions = win_ref.shape[1]
    centres = lax.broadcasted_iota(jnp.int32, (functions, 1), 0).astype(f32) * (
        REACH / (functions - 1)
    )
    envelope = jnp.square(1.0 - jnp.square(dist / CUTOFF))
    basis = jnp.exp(-jnp.square((dist - centres) / WIDTH_R)) * envelope
    pre = dot(win_ref[...], basis.astype(bf16))
    hidden = jnp.transpose(pre * (1.0 / (1.0 + jnp.exp(-pre)))).astype(bf16)
    for degree in range(degrees):
        lo = 2 * degree * channels
        rad[:, lo : lo + 2 * channels] = dot(hidden, wout_ref[:, lo : lo + 2 * channels])

    er = lax.broadcasted_iota(jnp.int32, (SUB, sub_edges), 0)
    el = lax.broadcasted_iota(jnp.int32, (SUB, sub_edges), 1)
    diag = jnp.where(lax.rem(el, SUB) == er, 1.0, 0.0)

    def gathered(first, count):
        return dot(hot, cand[:, first * channels : (first + count) * channels])

    def summed(values):
        return jnp.sum(values.reshape(subs, fanout, SUB, channels), axis=1)

    scalar = gathered(0, 1)
    cross = {}
    for degree in range(degrees):
        lo = (2 * degree + 1) * channels
        source = (rad[:, lo : lo + channels] * scalar).astype(bf16)
        members = range(degree * degree, (degree + 1) * (degree + 1))
        for s in range(subs):
            blocks = []
            for c in members:
                if c == 0:
                    blocks.append(diag)
                else:
                    blocks.append(diag * angular[c][:, s * sub_edges : (s + 1) * sub_edges])
            full = jnp.concatenate(blocks, axis=0)
            high = full.astype(bf16)
            low = (full - high.astype(f32)).astype(bf16)
            part_s = source[s * sub_edges : (s + 1) * sub_edges, :]
            value = dot(high, part_s) + dot(low, part_s)
            for i, c in enumerate(members):
                cross[(s, c)] = value[i * SUB : (i + 1) * SUB]
    norm = 1.0 / math.sqrt(fanout)
    c = 0
    while c < comps:
        count = min(2, comps - c)
        values = scalar if (c == 0 and count == 1) else gathered(c, count)
        for i in range(count):
            comp = c + i
            lo = 2 * degree_of(comp) * channels
            same = summed(values[:, i * channels : (i + 1) * channels] * rad[:, lo : lo + channels])
            total = jnp.concatenate([same[s] + cross[(s, comp)] for s in range(subs)], axis=0)
            agg[pl.ds(pl.multiple_of(step * ROWS, ROWS), ROWS), comp * channels : (comp + 1) * channels] = (
                total * norm
            ).astype(bf16)
        c += count

    @pl.when(step == pl.num_programs(0) - 1)
    def _():
        gates = dot(agg[:, 0:channels], wgate_ref[...])
        gates = 1.0 / (1.0 + jnp.exp(-gates))
        total = jnp.zeros((per_dev, wread_ref.shape[1]), f32)
        for comp in range(comps):
            degree = degree_of(comp)
            cols = slice(comp * channels, (comp + 1) * channels)
            own = own_ref[:, cols]
            mixed = dot(jnp.concatenate([agg[:, cols], own], axis=1), wcat_ref[degree])
            if degree == 0:
                new = own.astype(f32) + mixed * (1.0 / (1.0 + jnp.exp(-mixed)))
            else:
                new = own.astype(f32) + mixed * gates[:, (degree - 1) * channels : degree * channels]
            new = new.astype(bf16)
            out_ref[:, cols] = new
            total = total + dot(new, wread_ref[cols, :])
        coef[...] = total

        tile_col = tile_ref[...]
        pick = jnp.where(
            lax.broadcasted_iota(jnp.int32, (per_dev, tiles), 1) == tile_col, 1.0, 0.0
        )
        probes = [dot(pick, probe_ref[i], HIGH) - pos_ref[:, i : i + 1] for i in range(3)]
        for i in range(3):
            part[i] = probes[i]

        def body(t, carry):
            rows = pl.ds(pl.multiple_of(t * SUB, SUB), SUB)
            dist, ang = geometry(part[0, rows, :], part[1, rows, :], part[2, rows, :])
            co = coef[rows, :]
            envelope = jnp.square(1.0 - jnp.square(dist / CUTOFF))
            acc = jnp.zeros_like(dist)
            for b in range(functions):
                inner = jnp.broadcast_to(co[:, b : b + 1], dist.shape)
                for c in range(1, comps):
                    inner = inner + ang[c] * co[:, c * functions + b : c * functions + b + 1]
                centre = b * (REACH / (functions - 1))
                acc = acc + inner * jnp.exp(-jnp.square((dist - centre) / WIDTH_R))
            part[3, rows, :] = acc * envelope
            return carry

        lax.fori_loop(0, per_dev // SUB, body, 0)
        pick_t = jnp.transpose(jnp.where(
            lax.broadcasted_iota(jnp.int32, (per_dev, 128 * ((tiles + 127) // 128)), 1) == tile_col, 1.0, 0.0
        ))[0:tiles, :]
        dens_ref[...] = dot(pick_t, part[3], HIGH) * probe_ref[3] * scale


def swap(x, axis, partner):
    count = lax.axis_size(axis)
    return lax.ppermute(x, axis, [(i, partner(i, count)) for i in range(count)])


def low_partner(i, count):
    return i ^ 1


def high_partner(i, count):
    return (((i + 1) ^ 1) - 1) % count


def ring(x, axis):
    if lax.axis_size(axis) == 2:
        return [x, swap(x, axis, low_partner)]
    return [x, swap(x, axis, low_partner), swap(x, axis, high_partner)]


def ring_slot(offset, axis):
    if lax.axis_size(axis) == 2:
        return jnp.where(offset == 1, 0, 1)
    even = lax.axis_index(axis) % 2 == 0
    ahead = jnp.where(even, 1, 2)
    return jnp.where(offset == 1, 0, jnp.where(offset == 2, ahead, 3 - ahead))


def gather_plane(x):
    x = x[None]
    for axis in reversed(PLANE):
        count = lax.axis_size(axis)
        bit = 1
        while bit < count:
            other = swap(x, axis, lambda i, n, bit=bit: i ^ bit)
            up = (lax.axis_index(axis) // bit) % 2 == 1
            x = jnp.concatenate([jnp.where(up, other, x), jnp.where(up, x, other)], axis=0)
            bit *= 2
    return x


def scatter_plane(x):
    for axis in PLANE:
        count = lax.axis_size(axis)
        bit = count // 2
        while bit >= 1:
            half = x.shape[0] // 2
            up = (lax.axis_index(axis) // bit) % 2 == 1
            mine = jnp.where(up, x[half:], x[:half])
            theirs = jnp.where(up, x[:half], x[half:])
            x = mine + swap(theirs, axis, lambda i, n, bit=bit: i ^ bit)
            bit //= 2
    return x[0]


def per_device(
    features,
    positions,
    probe_positions,
    neighbours,
    routes,
    pattern,
    charge_index,
    charge_table,
    w_radial_in,
    w_radial_out,
    w_mix,
    w_self,
    w_gate,
    w_read,
):
    f32, bf16 = jnp.float32, jnp.bfloat16
    per_dev, comps, channels = features.shape
    degrees = w_mix.shape[0]
    functions = w_radial_in.shape[0]
    fanout = neighbours.shape[1]
    width = comps * channels
    rim = per_dev // 32
    probes = probe_positions.shape[1]

    levels = charge_table.shape[0]
    chosen = (jnp.arange(levels) == charge_index[0]).astype(f32)
    shift = jnp.sum(chosen[:, None] * charge_table.astype(f32), axis=0)

    def embed(block):
        flat = block.reshape(block.shape[0], width)
        scalar = (flat[:, :channels].astype(f32) + shift[None, :]).astype(bf16)
        return jnp.concatenate([scalar, flat[:, channels:]], axis=1)

    rim_pos = jnp.pad(positions[:, :rim].T, ((0, 0), (0, channels - 3)))
    message = jnp.concatenate([embed(features[:rim]), rim_pos], axis=1)
    message = jnp.concatenate(ring(message, "gz"), axis=0)
    message = jnp.concatenate(ring(message, "gy"), axis=0)
    ghosts = ring(message, "gx")
    if len(ghosts) == 2:
        ghosts.append(ghosts[1])
    rim_rows = message.shape[0]
    rim_pad = -(-rim_rows // 16) * 16

    own = embed(features)
    own_pos = jnp.pad(positions.T.astype(f32), ((0, 0), (0, channels - 3)))

    code = jnp.maximum(neighbours - per_dev, 0)
    cell = code // rim
    near_z = 2 if lax.axis_size("gz") == 2 else 3
    ghost_row = (
        per_dev
        + ring_slot(cell // 9, "gx") * rim_pad
        + (ring_slot(cell // 3 % 3, "gy") * near_z + ring_slot(cell % 3, "gz")) * rim
        + code % rim
    )
    index = jnp.where(neighbours < per_dev, neighbours, ghost_row).astype(jnp.int32)

    size_y, size_z = lax.axis_size("gy"), lax.axis_size("gz")
    tiles = size_y * size_z
    capacity = max(2, 2 * per_dev * routes.shape[1] // tiles)
    probe_blocks = pattern.shape[0]
    sheet = jnp.concatenate(
        [probe_positions.reshape(-1), pattern.astype(f32).reshape(-1)], axis=0
    )
    sheets = gather_plane(sheet)
    place = lax.axis_index("gy") * size_z + lax.axis_index("gz")
    probe_all = sheets[:, : 3 * probes].reshape(tiles, 3, probes)
    keep = lax.dynamic_index_in_dim(
        sheets[:, 3 * probes :].reshape(tiles, probe_blocks, tiles), place, axis=2, keepdims=False
    )
    keep = jnp.repeat(keep, probes // probe_blocks, axis=1)
    probe_all = jnp.concatenate([jnp.transpose(probe_all, (1, 0, 2)), keep[None]], axis=0)

    w_out = jnp.transpose(
        w_radial_out.reshape(-1, 2, degrees, channels), (0, 2, 1, 3)
    ).reshape(-1, 2 * degrees * channels)
    w_cat = jnp.concatenate([w_mix, w_self], axis=1)
    levels_of = [degree_of(c) for c in range(comps)]
    read = jnp.transpose(w_read, (1, 2, 0))[jnp.array(levels_of)]
    read = (read[:, :, None, :] * jnp.eye(comps, dtype=bf16)[:, None, :, None]).reshape(
        width, comps * functions
    )
    read_cols = -(-comps * functions // 128) * 128
    read = jnp.pad(read, ((0, 0), (0, read_cols - comps * functions)))

    kdim = per_dev + 3 * rim_pad
    sizes = (per_dev, channels, degrees, rim_rows, rim_pad, tiles, 1.0 / math.sqrt(tiles * capacity))
    whole = lambda *shape: pl.BlockSpec(shape, lambda i: (0,) * len(shape))
    new, partial = pl.pallas_call(
        functools.partial(layer_kernel, sizes),
        grid=(per_dev // ROWS,),
        out_shape=[
            jax.ShapeDtypeStruct((per_dev, width), bf16),
            jax.ShapeDtypeStruct((tiles, probes), f32),
        ],
        in_specs=[
            pl.BlockSpec((ROWS, fanout), lambda i: (i, 0)),
            whole(per_dev, width),
            whole(rim_rows, width + channels),
            whole(rim_rows, width + channels),
            whole(rim_rows, width + channels),
            whole(per_dev, channels),
            whole(w_radial_in.shape[1], functions),
            whole(*w_out.shape),
            whole(*w_cat.shape),
            whole(*w_gate.shape),
            whole(*read.shape),
            whole(*probe_all.shape),
            whole(per_dev, 1),
        ],
        out_specs=[whole(per_dev, width), whole(tiles, probes)],
        scratch_shapes=[
            pltpu.VMEM((kdim, width), bf16),
            pltpu.VMEM((SUB, kdim), bf16),
            pltpu.VMEM((per_dev, width), bf16),
            pltpu.VMEM((ROWS * fanout, 2 * degrees * channels), f32),
            pltpu.VMEM((per_dev, read_cols), f32),
            pltpu.VMEM((4, per_dev, probes), f32),
        ],
        compiler_params=pltpu.CompilerParams(vmem_limit_bytes=48 * 1024 * 1024),
    )(
        index,
        own,
        *ghosts,
        own_pos,
        w_radial_in.T,
        w_out,
        w_cat,
        w_gate,
        read,
        probe_all,
        routes,
    )
    density = scatter_plane(partial)
    return new.reshape(per_dev, comps, channels), density


def solution(mesh):
    split = ("gx", "gy", "gz")
    in_specs = (
        P(split, None, None),
        P(None, split),
        P(None, split),
        P(split, None),
        P(split, None),
        P(split, None),
    ) + (P(),) * 8
    out_specs = (P(split, None, None), P(split))
    return jax.shard_map(
        per_device, mesh=mesh, in_specs=in_specs, out_specs=out_specs, check_vma=False
    )
```
